1024 devices in a mesh: row: 32 (over x, y_lo, core), col: 32 (over z, y_hi).
Axes of the slice: x: 4, y: 8 (y_hi: 2, y_lo: 4; y = y_hi * 4 + y_lo), z: 16, core: 2. Of those that a mesh axis runs over, the one named last changes fastest.
Arguments:
- green: bfloat16 [4096, 57344], P('row', 'col'), may hold values from -0.0625 to 0.0625
- green_mask: int32 [32, 448], P('row', 'col'), may hold values 0 or 1
- tensor: bfloat16 [57344, 4096], P('row', 'col'), may hold values from -6 to 6
- tensor_mask: int32 [448, 32], P('row', 'col'), may hold values 0 or 1
Outputs:
- contracted: bfloat16 [4096, 4096], P('row', 'col')
The draws below stay inside these ranges and needn't reach their ends.
All inputs are finite; a program needn't handle non-finite values. No bound on the sum of `green_mask` or of `tensor_mask` on one device may be relied on, other than what follows from the above.
Results may differ from the reference program's by a relative error of at most 0.001.
Values may be sent and summed in bfloat16 or wider, within the bound.
A program may use at most 32 MiB of HBM per device.

```python
import jax
import jax.numpy as jnp
from jax import lax

LR = 128
RB = 1792
PB = 128
BLK = 128
WIN = 4
GROWS = 4096
GCOLS = 57344
TROWS = 57344
RICOLS = 4096
N_ROW = 32
N_COL = 32


def place_ends(result, own_key, least, high):
    place = [jax.random.randint(jax.random.fold_in(own_key, axis), (), 0, length) for axis, length in enumerate(result.shape)]
    widest = result.shape.index(max(result.shape))
    neighbour = place[:widest] + [(place[widest] + 1) % result.shape[widest]] + place[widest + 1:]
    return result.at[tuple(place)].set(least).at[tuple(neighbour)].set(high)


def block_scale(rng, dims, cuts, low, largest):
    def one(dim, parts):
        heights = jax.random.uniform(jax.random.fold_in(jax.random.fold_in(rng, 6), dim), (parts,), jnp.float32, low / len(cuts), largest / len(cuts))
        return jnp.repeat(jnp.exp(heights), dims[dim] // parts).reshape((-1,) + (1,) * (len(dims) - dim - 1))

    factor_of = one(*cuts[0])
    for cut in cuts[1:]:
        factor_of = factor_of * one(*cut)
    return factor_of


def normal_values(rng, dims, width, reach, cuts=(), kind=jnp.bfloat16):
    array = width * jax.random.normal(rng, dims, jnp.float32)
    if cuts:
        array = array * block_scale(rng, dims, cuts, -0.22, 0.18)
    return jnp.clip(array, -reach, reach).astype(kind)


def setup_inputs(seed: int = 0) -> dict:
    arg_keys = jax.random.split(jax.random.key(seed), 5)
    return {
        "green": normal_values(arg_keys[0], (GROWS, GCOLS), (WIN * RB) ** -0.5, 0.0625, ((0, 32), (1, 32))),
        "green_mask": place_ends((jax.random.randint(arg_keys[1], (GROWS // BLK, GCOLS // BLK), 0, 4) < 3).astype(jnp.int32), jax.random.fold_in(arg_keys[1], 1), 0, 1),
        "tensor": normal_values(arg_keys[2], (TROWS, RICOLS), 1.0, 6.0, ((0, 32), (1, 32))),
        "tensor_mask": place_ends((jax.random.randint(arg_keys[3], (TROWS // BLK, RICOLS // BLK), 0, 4) < 3).astype(jnp.int32), jax.random.fold_in(arg_keys[3], 1), 0, 1),
    }


def widen(mask, size):
    return jnp.repeat(jnp.repeat(mask, size, axis=0), size, axis=1)


def reference(green, green_mask, tensor, tensor_mask):
    green_kept = green * widen(green_mask, BLK).astype(green.dtype)
    tensor_kept = tensor * widen(tensor_mask, BLK).astype(tensor.dtype)
    per_col = N_ROW // N_COL
    green_tiles = green_kept.reshape(N_ROW, LR, N_ROW, RB)
    tile_ids = jnp.arange(N_ROW, dtype=jnp.int32)
    position = ((tile_ids % N_COL) * per_col + tile_ids // N_COL).astype(jnp.int32)
    green_ordered = jnp.take(green_tiles, position, axis=2)
    tensor_four = tensor_kept.reshape(N_ROW, RB, N_COL, PB)
    columns = jnp.arange(N_COL, dtype=jnp.int32)

    def row_block(index):
        total = jnp.zeros((LR, N_COL, PB), jnp.float32)
        green_row = lax.dynamic_index_in_dim(green_ordered, index, 0, keepdims=False)
        for step in range(WIN):
            picks = ((index + columns - step) % N_ROW).astype(jnp.int32)
            green_part = jnp.take(green_row, picks, axis=1).astype(jnp.float32)
            tensor_part = tensor_four[picks, :, columns, :].astype(jnp.float32)
            total = total + jnp.einsum("ajk,jkb->ajb", green_part, tensor_part, precision=lax.Precision.HIGHEST)
        return total

    blocks = lax.map(row_block, jnp.arange(N_ROW, dtype=jnp.int32))
    return blocks.reshape(N_ROW * LR, N_COL * PB).astype(jnp.bfloat16)
```

```python
import jax
import jax.numpy as jnp
from jax import lax
from jax.experimental import pallas as pl
from jax.experimental.pallas import tpu as pltpu
from jax.sharding import PartitionSpec as P

MESH = pl.DeviceIdType.MESH
BLK = 128
WHOLE = ((0, 1, 2), (4, 5, 6), (7, 8, 9), (11, 12, 13))
SHARED = (3, 3, 10, 10)
ROWS_FROM = (0, 64, 64, 0)
GP = 448
BP = 512
HALF = GP // 2
HOPS = 10


def kernel(green, gmask, tensor, tmask, out, gpart, bpart, z0, z1, z2a, z2b, z3, bx, by, acc, got, other,
           gx_send, gx_recv, bx_send, bx_recv, z_send, z_recv, y_send, y_recv, c_send, o_send, o_recv, h_send, h_recv):
    row, col = lax.axis_index("row"), lax.axis_index("col")
    x, low, core = row // 8, (row // 2) % 4, row % 2
    z, half = col // 2, col % 2
    y = 4 * half + low
    down = ((core - half) + 1) // 2
    up = ((half - core) + 1) // 2
    odd = down + up

    def at(x, y, z, core):
        return ((x * 4 + y % 4) * 2 + core, z * 2 + y // 4)

    z_up, z_down = at(x, y, (z + 1) % 16, core), at(x, y, (z + 15) % 16, core)
    mate = at(x, y, z, 1 - core)
    barrier = pltpu.get_barrier_semaphore()
    friends = [at((x + d) % 4, y, z, core) for d in (1, 2, 3)]
    friends += [at(x, (y + d) % 8, z, core) for d in range(1, 8)]
    friends += [z_up, z_down, mate]
    for friend in friends:
        pl.semaphore_signal(barrier, inc=1, device_id=friend, device_id_type=MESH)

    def kept_green(b, first, count):
        scale = gmask[0, b].astype(jnp.float32)
        return (green[pl.ds(first, count), b * BLK:(b + 1) * BLK].astype(jnp.float32) * scale).astype(jnp.bfloat16)

    def kept_tensor(b):
        scale = tmask[b, 0].astype(jnp.float32)
        return (tensor[b * BLK:(b + 1) * BLK, :].astype(jnp.float32) * scale).astype(jnp.bfloat16)

    for q in range(4):
        for n, b in enumerate(WHOLE[q]):
            gpart[q, n * BLK:(n + 1) * BLK, :] = kept_green(b, 0, BLK)
        gpart[q, 3 * BLK:GP, :] = kept_green(SHARED[q], ROWS_FROM[q], 64)
    for q in range(4):
        for n, b in enumerate(WHOLE[q] + (SHARED[q],)):
            bpart[q, n * BLK:(n + 1) * BLK, :] = kept_tensor(b)

    pl.semaphore_wait(barrier, len(friends))

    def remote(src, dst, send, recv, device):
        return pltpu.make_async_remote_copy(src_ref=src, dst_ref=dst, send_sem=send, recv_sem=recv,
                                            device_id=device, device_id_type=MESH)

    lands = (
        ((z0.at[4], 0, GP, 0),),
        ((z1.at[0], 0, GP, 1),),
        ((z2a.at[0], 0, HALF, 2), (z2b.at[0], HALF, HALF, 3)),
        ((z3.at[0], 0, GP, 4),),
    )
    for p in range(4):
        @pl.when(x == p)
        def _():
            for d in (2, 1, 3):
                q = (p + d) % 4
                for dst, first, count, s in lands[p]:
                    remote(gpart.at[q, pl.ds(first, count)], dst, gx_send.at[d, s], gx_recv.at[s], at(q, y, z, core)).start()
            for dst, first, count, s in lands[p]:
                pltpu.make_async_copy(gpart.at[p, pl.ds(first, count)], dst, gx_recv.at[s]).start()
    pltpu.make_async_copy(bpart.at[x], bx.at[x], bx_recv.at[x]).start()
    for d in (2, 1, 3):
        q = (x + d) % 4
        remote(bpart.at[q], bx.at[x], bx_send.at[d], bx_recv.at[x], at(q, y, z, core)).start()

    far_down = jnp.where(low < 2, 1, 0)
    n2b = 9 - low + up
    n2a = jnp.where(low < 2, 8 + low + down, n2b)
    n0d, n0u = low + down, jnp.maximum(1 + up - low, 0)
    n1, n3 = low + 4 + down, 5 - low + up

    def step(number, hops, slot, device, t):
        @pl.when(jnp.logical_and(t >= 1, t <= hops))
        def _():
            remote(slot(t), slot(t), z_send.at[number, t], z_recv.at[number, t], device).wait_recv()

        @pl.when(t < hops)
        def _():
            remote(slot(t), slot(t + 1), z_send.at[number, t + 1], z_recv.at[number, t + 1], device).start()

    a_row = (x * 4 + low) * 2 + core
    a_device = (a_row, jnp.where(low < 2, (z + 15) % 16, (z + 1) % 16) * 2 + half)
    conveyors = (
        (0, n2a, lambda t: z2a.at[t], a_device),
        (1, n2b, lambda t: z2b.at[t], z_up),
        (2, n1, lambda t: z1.at[t], z_down),
        (3, n3, lambda t: z3.at[t], z_up),
        (4, n0d, lambda t: z0.at[4 - t], z_down),
        (5, n0u, lambda t: z0.at[4 + t], z_up),
    )
    for p in range(4):
        for dst, first, count, s in lands[p]:
            pltpu.make_async_copy(dst, dst, gx_recv.at[s]).wait()
    for conveyor in conveyors:
        step(*conveyor, 0)

    for p in range(4):
        pltpu.make_async_copy(bx.at[p], bx.at[p], bx_recv.at[p]).wait()

    def target(e):
        return 4 * core + (low - z + e + 16) % 4

    def send_y(e):
        device_y = target(e)

        @pl.when(device_y == y)
        def _():
            pltpu.make_async_copy(bx, by.at[half, e + 1], y_recv.at[half, e + 1]).start()

        @pl.when(device_y != y)
        def _():
            remote(bx, by.at[half, e + 1], y_send.at[e + 1], y_recv.at[half, e + 1], at(x, device_y, z, core)).start()

    def sent_y(e):
        device_y = target(e)

        @pl.when(device_y != y)
        def _():
            remote(bx, by.at[half, e + 1], y_send.at[e + 1], y_recv.at[half, e + 1], at(x, device_y, z, core)).wait_send()

    extra = 3 * core - 1
    send_y(0)
    send_y(1)

    @pl.when(odd == 1)
    def _():
        send_y(extra)

    def later(t, carry):
        for conveyor in conveyors:
            step(*conveyor, t)
        return carry

    lax.fori_loop(1, HOPS + 1, later, 0)

    def have(hj, e):
        pltpu.make_async_copy(bx, by.at[hj, e + 1], y_recv.at[hj, e + 1]).wait()

    def hand(hj, e):
        return remote(by.at[hj, e + 1], by.at[hj, e + 1], c_send.at[hj, e + 1], y_recv.at[hj, e + 1], mate)

    for h in range(2):
        pieces = ((1, 0), (0, 1), (1, 1), (0, 2)) if h else ((1, -1), (0, 0), (1, 0), (0, 1))
        alone = (0, 0) if h else (1, 1)

        @pl.when(jnp.logical_and(half == h, core == h))
        def _():
            for piece in pieces:
                have(*piece)
                hand(*piece).start()
            have(*alone)

        @pl.when(jnp.logical_and(half == h, core != h))
        def _():
            for piece in pieces:
                have(*piece)

    acc[...] = jnp.zeros_like(acc)
    shared_rows = 64 * ((x * (3 - x)) // 2)
    for n in range(3):
        e = n - down

        def products():
            for p in range(4):
                if p == 0:
                    part = z0[4 - low + e]
                elif p == 1:
                    part = z1[4 + low - e]
                elif p == 2:
                    hop = 8 - low + e
                    part = jnp.concatenate([z2a[jnp.where(low < 2, 8 + low - e, hop)], z2b[hop]], axis=0)
                else:
                    part = z3[4 - low + e]
                wide = jnp.concatenate([part[:BLK], part[BLK:2 * BLK], part[2 * BLK:3 * BLK]], axis=1)
                rest = part[3 * BLK:]
                place = ((low + 4 * p + z - e + 16) % 16) // 4
                for hj in range(2):
                    s = core + hj - half + 2 * e

                    @pl.when(jnp.logical_and(s >= 0, s <= 3))
                    def _():
                        block = by[hj, e + 1, place, :3 * BLK]
                        last = by[hj, e + 1, place, 3 * BLK:]
                        acc[p, hj] += jnp.dot(wide, block, preferred_element_type=jnp.float32)
                        acc[p, hj, pl.ds(pl.multiple_of(shared_rows, 64), 64)] += jnp.dot(
                            rest, last, preferred_element_type=jnp.float32)

        if n < 2:
            products()
        else:
            pl.when(odd == 1)(products)

    def give(d):
        q = (x + d) % 4
        return remote(acc.at[q], got.at[x], o_send.at[d], o_recv.at[x], at(q, y, z, core))

    for d in (2, 1, 3):
        give(d).start()
    for d in (1, 3, 2):
        p = (x + d) % 4
        pltpu.make_async_copy(got.at[p], got.at[p], o_recv.at[p]).wait()
        acc[x] += got[p]
    swap = remote(acc.at[x, 1 - half], other, h_send, h_recv, at(x, (y + 4) % 8, z, core))
    swap.start()
    swap.wait_recv()
    out[...] = (acc[x, half] + other[...]).astype(jnp.bfloat16)

    swap.wait_send()
    for d in (1, 2, 3):
        give(d).wait_send()
        remote(bpart.at[x], bx.at[x], bx_send.at[d], bx_recv.at[x], mate).wait_send()
    for p in range(4):
        @pl.when(x == p)
        def _():
            for d in (1, 2, 3):
                for dst, first, count, s in lands[p]:
                    remote(gpart.at[p, pl.ds(first, count)], dst, gx_send.at[d, s], gx_recv.at[s], mate).wait_send()
    sent_y(0)
    sent_y(1)

    @pl.when(odd == 1)
    def _():
        sent_y(extra)

    for h in range(2):
        pieces = ((1, 0), (0, 1), (1, 1), (0, 2)) if h else ((1, -1), (0, 0), (1, 0), (0, 1))

        @pl.when(jnp.logical_and(half == h, core == h))
        def _():
            for piece in pieces:
                hand(*piece).wait_send()

    def drain(t, carry):
        for number, hops, slot, device in conveyors:
            @pl.when(t < hops)
            def _():
                remote(slot(t), slot(t + 1), z_send.at[number, t + 1], z_recv.at[number, t + 1], device).wait_send()
        return carry

    lax.fori_loop(0, HOPS, drain, 0)


def shards(green, green_mask, tensor, tensor_mask):
    vmem, smem = pl.BlockSpec(memory_space=pltpu.VMEM), pl.BlockSpec(memory_space=pltpu.SMEM)
    half, single, dma = jnp.bfloat16, jnp.float32, pltpu.SemaphoreType.DMA
    return pl.pallas_call(
        kernel,
        name="window",
        out_shape=jax.ShapeDtypeStruct((BLK, BLK), half),
        in_specs=[vmem, smem, vmem, smem],
        out_specs=vmem,
        scratch_shapes=[
            pltpu.VMEM((4, GP, BLK), half), pltpu.VMEM((4, BP, BLK), half),
            pltpu.VMEM((7, GP, BLK), half), pltpu.VMEM((9, GP, BLK), half),
            pltpu.VMEM((HOPS + 1, HALF, BLK), half), pltpu.VMEM((HOPS + 1, HALF, BLK), half),
            pltpu.VMEM((7, GP, BLK), half),
            pltpu.VMEM((4, BP, BLK), half), pltpu.VMEM((2, 4, 4, BP, BLK), half),
            pltpu.VMEM((4, 2, BLK, BLK), single), pltpu.VMEM((4, 2, BLK, BLK), single), pltpu.VMEM((BLK, BLK), single),
            dma((4, 5)), dma((5,)), dma((4,)), dma((4,)), dma((6, HOPS + 1)), dma((6, HOPS + 1)),
            dma((4,)), dma((2, 4)), dma((2, 4)), dma((4,)), dma((4,)), dma, dma,
        ],
        compiler_params=pltpu.CompilerParams(collective_id=0, has_side_effects=True, vmem_limit_bytes=40 << 20),
        cost_estimate=pl.CostEstimate(flops=8 * BLK * BLK * 1792, bytes_accessed=2 * 2 * BLK * 1792, transcendentals=0),
    )(green, green_mask, tensor, tensor_mask)


def solution(mesh):
    spec = P("row", "col")
    return jax.shard_map(shards, mesh=mesh, in_specs=(spec,) * 4, out_specs=spec, check_vma=False)
```

```python
import jax
import jax.numpy as jnp
from jax import lax
from jax.experimental import pallas as pl
from jax.experimental.pallas import tpu as pltpu
from jax.sharding import PartitionSpec as P

MESH = pl.DeviceIdType.MESH
BLK = 128
SUB = 64
WIDTH = 14 * BLK
WHOLE = ((0, 1, 2), (4, 5, 6), (7, 8, 9), (11, 12, 13))
SHARED = (3, 3, 10, 10)
LAST = (0, 1, 0, 1)
PART = 3 * BLK + SUB
CUTS = ((0, 112), (112, 224), (336, 112))
Z_HOPS = 10
Y_HOPS = 5
ORDER = (0, 1, 3, 2)
HOP_CODES = (
    (
        ((0x828049, 0x940049), (0x920003, 0x228003), (0x740013, 0x920013), (0x880052, 0x740052)),
        ((0x144600, 0x024600), (0x014248, 0xb44248), (0x02b488, 0x014488), (0x124680, 0x02b680)),
    ),
    (
        ((0x800a49, 0x880a49), (0x900000, 0x968003), (0x6c0013, 0x920013), (0x880052, 0x758052)),
        ((0x16c000, 0x124000), (0x02c24d, 0x004248), (0x0eb488, 0x014488), (0x124680, 0x01b680)),
    ),
)


def kernel(green_hbm, gmask, tensor_hbm, tmask, out, green, tensor, gpart, bpart, z0, z1, z2a, z2b, z2c, z3, by, acc, got,
           in_sem, gx_send, gx_recv, bx_send, z_send, z_recv, y_send, y_recv, c_send, c_recv, o_send, o_recv):
    row, col = lax.axis_index("row"), lax.axis_index("col")
    x, low, core = row // 8, (row // 2) % 4, row % 2
    z, half = col // 2, col % 2
    y = 4 * half + low
    down = ((core - half) + 1) // 2
    up = ((half - core) + 1) // 2
    odd = down + up

    def at(x, y, z, core):
        return ((x * 4 + y % 4) * 2 + core, z * 2 + y // 4)

    def remote(src, dst, send, recv, device):
        return pltpu.make_async_remote_copy(src_ref=src, dst_ref=dst, send_sem=send, recv_sem=recv,
                                            device_id=device, device_id_type=MESH)

    z_up, z_down = at(x, y, (z + 1) % 16, core), at(x, y, (z + 15) % 16, core)
    def picked(*cases):
        chosen = 0
        for case_low, case_half in cases:
            chosen = chosen + jnp.where(jnp.logical_and(low == case_low, half == case_half), 1, 0)
        return chosen

    a_down = picked((0, 1), (1, 0))
    b_down = picked((0, 0), (0, 1), (1, 1))
    far_up, far_down = 9 - low + up, 8 + low + down
    n0d, n0u = low + down, jnp.maximum(1 + up - low, 0)
    n1, n3 = low + 4 + down, 5 - low + up

    mate = at(x, y, z, 1 - core)
    load_green = pltpu.make_async_copy(green_hbm, green, in_sem.at[0])
    load_tensor = pltpu.make_async_copy(tensor_hbm, tensor, in_sem.at[1])
    load_green.start()
    load_tensor.start()
    barrier = pltpu.get_barrier_semaphore()
    friends = [at((x + d) % 4, y, z, core) for d in (1, 2, 3)]
    friends += [at((x + d) % 4, (y + 4) % 8, z, core) for d in (1, 2, 3)]
    friends += [at(x, (y + d) % 8, z, core) for d in range(1, 8)]
    friends += [at(x, y, (z - way * jnp.maximum(hops - 1 - odd, 1) + 16) % 16, core) for hops, way in (
        (jnp.where(b_down == 1, far_down, far_up), 1 - 2 * b_down), (jnp.where(a_down == 1, far_down, far_up), 1 - 2 * a_down),
        (far_up, 1), (n1, -1), (n3, 1), (n0d, -1))]
    friends += [z_up, z_down, mate]
    for friend in friends:
        pl.semaphore_signal(barrier, inc=1, device_id=friend, device_id_type=MESH)

    load_tensor.wait()
    for q in range(4):
        for n, b in enumerate(WHOLE[q]):
            scale = tmask[b, 0].astype(jnp.float32)
            block = tensor[b * BLK:(b + 1) * BLK, :].astype(jnp.float32)
            bpart[q, n * BLK:(n + 1) * BLK, :] = (block * scale).astype(jnp.bfloat16)
        b = SHARED[q]
        first = b * BLK + SUB * LAST[q]
        block = tensor[first:first + SUB, :].astype(jnp.float32) * tmask[b, 0].astype(jnp.float32)
        bpart[q, 3 * BLK:, :] = block.astype(jnp.bfloat16)
    pl.semaphore_wait(barrier, len(friends))
    pltpu.make_async_copy(bpart.at[x], by.at[y, x], y_recv.at[y, x]).start()
    for d in (2, 1, 3):
        q = (x + d) % 4
        remote(bpart.at[q], by.at[y, x], bx_send.at[d], y_recv.at[y, x], at(q, y, z, core)).start()


    load_green.wait()
    left = lax.broadcasted_iota(jnp.int32, (SUB, BLK), 1) < SUB
    for q in range(4):
        for n, b in enumerate(WHOLE[q]):
            scale = gmask[0, b].astype(jnp.float32)
            block = green[:, b * BLK:(b + 1) * BLK].astype(jnp.float32)
            gpart[q, n * BLK:(n + 1) * BLK, :] = (block * scale).astype(jnp.bfloat16)
        b = SHARED[q]
        block = green[:, b * BLK:(b + 1) * BLK].astype(jnp.float32) * gmask[0, b].astype(jnp.float32)
        top, bottom = block[:SUB], block[SUB:]
        if LAST[q]:
            both = jnp.where(left, pltpu.roll(top, SUB, 1), bottom)
        else:
            both = jnp.where(left, top, pltpu.roll(bottom, SUB, 1))
        gpart[q, 3 * BLK:, :] = both.astype(jnp.bfloat16)

    lands = (
        ((z0.at[4], 0, PART, 0),),
        ((z1.at[0], 0, PART, 1),),
        tuple((ref.at[0], *cut, 2 + n) for n, (ref, cut) in enumerate(zip((z2a, z2b, z2c), CUTS))),
        ((z3.at[0], 0, PART, 5),),
    )
    for p in range(4):
        @pl.when(x == p)
        def _():
            for dst, first, count, s in lands[p]:
                pltpu.make_async_copy(gpart.at[p, pl.ds(first, count)], dst, gx_recv.at[s]).start()
            for d in (2, 1, 3):
                q = (p + d) % 4
                for dst, first, count, s in lands[p]:
                    remote(gpart.at[q, pl.ds(first, count)], dst, gx_send.at[d, s], gx_recv.at[s], at(q, y, z, core)).start()

    conveyors = (
        (1, 2, jnp.where(b_down == 1, far_down, far_up), lambda t: z2b.at[t], 1 - 2 * b_down),
        (0, 2, jnp.where(a_down == 1, far_down, far_up), lambda t: z2a.at[t], 1 - 2 * a_down),
        (2, 2, far_up, lambda t: z2c.at[t], 1),
        (3, 1, n1, lambda t: z1.at[t], -1),
        (4, 3, n3, lambda t: z3.at[t], 1),
        (5, 0, n0d, lambda t: z0.at[4 - t], -1),
        (6, 0, n0u, lambda t: z0.at[4 + t], 1),
    )

    def jump_of(hops):
        return jnp.maximum(hops - 1 - odd, 0)

    def hop(number, slot, way, t, by_hops):
        device = at(x, y, (z + way * by_hops + 16) % 16, core)
        return remote(slot(t), slot(t + by_hops), z_send.at[number, t + by_hops], z_recv.at[number, t + by_hops], device)

    def z_first(p):
        for dst, first, count, s in lands[p]:
            pltpu.make_async_copy(dst, dst, gx_recv.at[s]).wait()
        for number, part, hops, slot, way in conveyors:
            if part == p:
                @pl.when(hops > 0)
                def _():
                    hop(number, slot, way, 0, jnp.maximum(jump_of(hops), 1)).start()

    def z_step(step, parts):
        for number, part, hops, slot, way in conveyors:
            t = jump_of(hops) + step
            if part in parts:
                @pl.when(jnp.logical_and(t > 0, t <= hops))
                def _():
                    hop(number, slot, way, t - 1, 1).wait_recv()

                    @pl.when(t < hops)
                    def _():
                        hop(number, slot, way, t, 1).start()

    def codes_of(pair, way):
        code = 0
        for m in range(4):
            for c in range(2):
                here = jnp.logical_and(z % 4 == m, core == c)
                code = code + jnp.where(here, HOP_CODES[pair][way][m][c], 0)
        return code

    codes = tuple(tuple(codes_of(pair, way) for way in range(2)) for pair in range(2))

    def y_hops(pair, way, o):
        return lax.shift_right_logical(codes[pair][way], 3 * ((o + 4 * core) % 8)) % 8

    def wanted(way, o, t):
        origin = (o + 4 * core) % 8
        place = (origin + (t if way == 0 else 8 - t)) % 8
        e = (place - origin + z + 16) % 4
        third = jnp.logical_and(origin >= 4, e == 3 - core)
        return jnp.logical_and(place < 4, jnp.logical_or(e < 2, third))

    def y_hop(way, t, o, p, hops):
        by_hops = hops - t
        for d in (4, 3, 2, 1):
            by_hops = jnp.where(jnp.logical_and(t + d <= hops, wanted(way, o, t + d)), d, by_hops)
        device = at(x, (y + (by_hops if way == 0 else 8 - by_hops)) % 8, z, core)
        return remote(by.at[o, p], by.at[o, p], y_send.at[way, t, p], y_recv.at[o, p], device)

    e_mate = (2 * half - 1 - 1) // 2

    def piece_of(o):
        return 2 * ((low + z - e_mate - o % 4 + 16) % 4) + o // 4 - 1

    def hand(o, p):
        piece = piece_of(o)
        return remote(by.at[o, p], by.at[8 + piece, p], c_send.at[o, p], c_recv.at[piece, p], mate)

    def handed(o):
        piece = piece_of(o)
        return jnp.logical_and(core == half, jnp.logical_and(piece >= 0, piece <= 3))

    def y_step(a, t):
        p = (x + ORDER[a]) % 4

        def arrived(o):
            pltpu.make_async_copy(by.at[o, p], by.at[o, p], y_recv.at[o, p]).wait()

        @pl.when(t == 0)
        def _():
            arrived(y)
            for way in range(2):
                hops = y_hops(a // 2, way, y)

                @pl.when(hops > 0)
                def _():
                    y_hop(way, 0, y, p, hops).start()

            @pl.when(jnp.logical_and(handed(y), half == core))
            def _():
                hand(y, p).start()

        @pl.when(jnp.logical_and(t > 0, t <= Y_HOPS))
        def _():
            for way in range(2):
                o = (y + (8 - t if way == 0 else t)) % 8
                hops = y_hops(a // 2, way, o)

                @pl.when(jnp.logical_and(hops >= t, wanted(way, o, t)))
                def _():
                    arrived(o)

                    @pl.when(hops > t)
                    def _():
                        y_hop(way, t, o, p, hops).start()

                    @pl.when(handed(o))
                    def _():
                        hand(o, p).start()

    y_step(0, 0)
    for p in range(4):
        pl.when(x == p)(lambda p=p: z_first(p))

    def y_all(t, carry):
        for a in range(4):
            y_step(a, t - a)

        @pl.when(t == 2)
        def _():
            for p in range(4):
                pl.when(x != p)(lambda p=p: z_first(p))

        @pl.when(t == 5)
        def _():
            z_step(0, (0, 3))

        @pl.when(t == 6)
        def _():
            z_step(0, (1,))
            z_step(1, (0, 3))

        @pl.when(t == 7)
        def _():
            z_step(0, (2,))
            z_step(1, (1,))
            z_step(2, (0, 3))

        return carry

    lax.fori_loop(1, Y_HOPS + 4, y_all, 0)

    @pl.when(odd == 1)
    def _():
        for piece in range(4):
            for p in range(4):
                pltpu.make_async_copy(by.at[8 + piece, p], by.at[8 + piece, p], c_recv.at[piece, p]).wait()

    acc[...] = jnp.zeros_like(acc)
    nothing = jnp.zeros((SUB, BLK), jnp.bfloat16)

    def one(p, n):
        e = n - down
        if p == 0:
            part = z0[4 - low + e]
        elif p == 1:
            part = z1[4 + low - e]
        elif p == 2:
            h_up, h_down = 8 - low + e, 8 + low - e
            part = jnp.concatenate([z2a[jnp.where(a_down == 1, h_down, h_up)], z2b[jnp.where(b_down == 1, h_down, h_up)],
                                    z2c[h_up]], axis=0)
        else:
            part = z3[4 - low + e]
        wide = jnp.concatenate([part[:BLK], part[BLK:2 * BLK], part[2 * BLK:3 * BLK]], axis=1)
        rest = part[3 * BLK:]
        place = ((low + 4 * p + z - e + 16) % 16) // 4
        for hj in range(2):
            s = core + hj - half + 2 * e

            @pl.when(jnp.logical_and(s >= 0, s <= 3))
            def _():
                where = jnp.where(odd == 1, 8 + 2 * n + hj - 1, 4 * hj + (low + z - e + 16) % 4)
                other = by[where, place]
                last = other[3 * BLK:]
                ends = jnp.concatenate([jnp.concatenate([last, nothing], axis=0), jnp.concatenate([nothing, last], axis=0)], axis=1)
                total = jnp.dot(wide, other[:3 * BLK], preferred_element_type=jnp.float32)
                pair = jnp.dot(rest, ends, preferred_element_type=jnp.float32)
                acc[p, hj] += total + jnp.concatenate([pair[:, :BLK], pair[:, BLK:]], axis=0)

    def give(p, hj):
        return remote(acc.at[p, hj], got.at[2 * x + hj], o_send.at[p, hj], o_recv.at[2 * x + hj], at(p, y, z, core))

    def give_last(hj):
        return remote(acc.at[2, hj], got.at[2 * x + half], o_send.at[2, hj], o_recv.at[2 * x + half], at(2, 4 * hj + low, z, core))

    swap = remote(acc.at[x, 1 - half], got.at[8], o_send.at[x, half], o_recv.at[8], at(x, (y + 4) % 8, z, core))

    def took(n):
        pltpu.make_async_copy(got.at[n], got.at[n], o_recv.at[n]).wait()

    def products(p):
        one(p, 0)
        one(p, 1)

        @pl.when(odd == 1)
        def _():
            one(p, 2)

        for hj in range(2):
            if p == 2:
                @pl.when(jnp.logical_or(x != 2, half != hj))
                def _():
                    give_last(hj).start()
            else:
                @pl.when(x != p)
                def _():
                    give(p, hj).start()

    def sum_x():
        for d in (1, 3, 2):
            for hj in range(2):
                n = 2 * ((x + d) % 4) + hj
                took(n)
                acc[x, hj] += got[n]
        swap.start()

    products(0)
    products(3)
    z_step(1, (2,))
    z_step(2, (1,))
    products(1)
    z_step(2, (2,))
    products(2)
    pl.when(x != 2)(sum_x)

    @pl.when(x != 2)
    def _():
        took(8)
        out[...] = (acc[x, half] + got[8]).astype(jnp.bfloat16)

    @pl.when(x == 2)
    def _():
        total = acc[2, half]
        for d in range(1, 8):
            n = (4 + half + d) % 8
            took(n)
            total = total + got[n]
        out[...] = total.astype(jnp.bfloat16)

    for p in range(4):
        for hj in range(2):
            if p == 2:
                @pl.when(jnp.logical_or(x != 2, half != hj))
                def _():
                    give_last(hj).wait_send()
            else:
                @pl.when(x != p)
                def _():
                    give(p, hj).wait_send()

        @pl.when(x == p)
        def _():
            for d in (1, 2, 3):
                for dst, first, count, s in lands[p]:
                    remote(gpart.at[p, pl.ds(first, count)], dst, gx_send.at[d, s], gx_recv.at[s], mate).wait_send()
    for d in (1, 2, 3):
        remote(bpart.at[x], by.at[y, x], bx_send.at[d], y_recv.at[y, x], mate).wait_send()

    pl.when(x != 2)(swap.wait_send)
    for number, part, hops, slot, way in conveyors:
        jump = jump_of(hops)

        @pl.when(hops > 0)
        def _():
            hop(number, slot, way, 0, jnp.maximum(jump, 1)).wait_send()

        for step in range(3):
            t = jump + step

            @pl.when(jnp.logical_and(t > 0, t < hops))
            def _():
                hop(number, slot, way, t, 1).wait_send()

    def drain(t, carry):
        for a in range(4):
            p = (x + ORDER[a]) % 4
            for way in range(2):
                o = (y + (8 - t if way == 0 else t)) % 8
                hops = y_hops(a // 2, way, o)

                @pl.when(jnp.logical_and(hops > t, jnp.logical_or(t == 0, wanted(way, o, t))))
                def _():
                    y_hop(way, t, o, p, hops).wait_send()

                reached = hops >= t if way == 0 else jnp.logical_and(hops >= t, t > 0)

                @pl.when(jnp.logical_and(handed(o), reached))
                def _():
                    hand(o, p).wait_send()
        return carry

    lax.fori_loop(0, Y_HOPS + 1, drain, 0)


def shards(green, green_mask, tensor, tensor_mask):
    vmem, smem, hbm = (pl.BlockSpec(memory_space=space) for space in (pltpu.VMEM, pltpu.SMEM, pltpu.HBM))
    half, single, dma = jnp.bfloat16, jnp.float32, pltpu.SemaphoreType.DMA
    slots = Z_HOPS + 1
    return pl.pallas_call(
        kernel,
        name="window",
        out_shape=jax.ShapeDtypeStruct((BLK, BLK), half),
        in_specs=[hbm, smem, hbm, smem],
        out_specs=vmem,
        scratch_shapes=[
            pltpu.VMEM((BLK, WIDTH), half), pltpu.VMEM((WIDTH, BLK), half),
            pltpu.VMEM((4, PART, BLK), half), pltpu.VMEM((4, PART, BLK), half),
            pltpu.VMEM((7, PART, BLK), half), pltpu.VMEM((9, PART, BLK), half),
            *(pltpu.VMEM((slots, count, BLK), half) for _, count in CUTS),
            pltpu.VMEM((7, PART, BLK), half), pltpu.VMEM((12, 4, PART, BLK), half),
            pltpu.VMEM((4, 2, BLK, BLK), single), pltpu.VMEM((9, BLK, BLK), single),
            dma((2,)), dma((4, 6)), dma((6,)), dma((4,)), dma((7, slots)), dma((7, slots)),
            dma((2, Y_HOPS + 1, 4)), dma((8, 4)), dma((8, 4)), dma((4, 4)), dma((4, 2)), dma((9,)),
        ],
        compiler_params=pltpu.CompilerParams(collective_id=0, has_side_effects=True, vmem_limit_bytes=60 << 20),
        cost_estimate=pl.CostEstimate(flops=8 * BLK * BLK * WIDTH, bytes_accessed=4 * BLK * WIDTH, transcendentals=0),
    )(green, green_mask, tensor, tensor_mask)


def solution(mesh):
    spec = P("row", "col")
    return jax.shard_map(shards, mesh=mesh, in_specs=(spec,) * 4, out_specs=spec, check_vma=False)
```

```python
import jax
import jax.numpy as jnp
from jax import lax
from jax.experimental import pallas as pl
from jax.experimental.pallas import tpu as pltpu
from jax.sharding import PartitionSpec as P

MESH = pl.DeviceIdType.MESH
BLK = 128
SUB = 64
WIDTH = 14 * BLK
WHOLE = ((0, 1, 2), (4, 5, 6), (7, 8, 9), (11, 12, 13))
SHARED = (3, 3, 10, 10)
LAST = (0, 1, 0, 1)
PART = 3 * BLK + SUB
CUTS = ((0, 112), (112, 224), (336, 112))
Z_HOPS = 10
Y_HOPS = 5
ORDER = (0, 1, 3, 2)
DIRECT = (1, 2)
HOP_CODES = (
    (
        ((0x828049, 0x940049), (0x920003, 0x228003), (0x740013, 0x920013), (0x880052, 0x740052)),
        ((0x144600, 0x024600), (0x014248, 0xb44248), (0x02b488, 0x014488), (0x124680, 0x02b680)),
    ),
    (
        ((0x800a49, 0x880a49), (0x900000, 0x968003), (0x6c0013, 0x920013), (0x880052, 0x758052)),
        ((0x16c000, 0x124000), (0x02c24d, 0x004248), (0x0eb488, 0x014488), (0x124680, 0x01b680)),
    ),
)


def kernel(green_hbm, gmask, tensor_hbm, tmask, out, green, tensor, gpart, bpart, z0, z1, z2a, z2b, z2c, z3, by, acc, got,
           in_sem, gx_send, gx_recv, bx_send, z_send, z_recv, y_send, y_recv, c_send, c_recv, o_send, o_recv):
    row, col = lax.axis_index("row"), lax.axis_index("col")
    x, low, core = row // 8, (row // 2) % 4, row % 2
    z, half = col // 2, col % 2
    y = 4 * half + low
    down = ((core - half) + 1) // 2
    up = ((half - core) + 1) // 2
    odd = down + up

    def at(x, y, z, core):
        return ((x * 4 + y % 4) * 2 + core, z * 2 + y // 4)

    def remote(src, dst, send, recv, device):
        return pltpu.make_async_remote_copy(src_ref=src, dst_ref=dst, send_sem=send, recv_sem=recv,
                                            device_id=device, device_id_type=MESH)

    z_up, z_down = at(x, y, (z + 1) % 16, core), at(x, y, (z + 15) % 16, core)
    def picked(*cases):
        chosen = 0
        for case_low, case_half in cases:
            chosen = chosen + jnp.where(jnp.logical_and(low == case_low, half == case_half), 1, 0)
        return chosen

    a_down = picked((0, 1), (1, 0)) + (1 - core) * picked((2, 1))
    b_down = picked((0, 0), (0, 1), (1, 1))
    far_up, far_down = 9 - low + up, 8 + low + down
    n0d, n0u = low + down, jnp.maximum(1 + up - low, 0)
    n1, n3 = low + 4 + down, 5 - low + up

    mate = at(x, y, z, 1 - core)
    load_green = pltpu.make_async_copy(green_hbm, green, in_sem.at[0])
    load_tensor = pltpu.make_async_copy(tensor_hbm, tensor, in_sem.at[1])
    load_green.start()
    load_tensor.start()
    barrier = pltpu.get_barrier_semaphore()
    friends = [at((x + d) % 4, y, z, core) for d in (1, 2, 3)]
    friends += [at((x + d) % 4, (y + 4) % 8, z, core) for d in (1, 2, 3)]
    friends += [at(x, (y + d) % 8, z, core) for d in range(1, 8)]
    friends += [at(x, y, (z - way * jnp.maximum(hops - 1 - odd, 1) + 16) % 16, core) for hops, way in (
        (jnp.where(b_down == 1, far_down, far_up), 1 - 2 * b_down), (jnp.where(a_down == 1, far_down, far_up), 1 - 2 * a_down),
        (far_up, 1), (n1, -1), (n3, 1), (n0d, -1))]
    friends += [z_up, z_down, mate]
    for friend in friends:
        pl.semaphore_signal(barrier, inc=1, device_id=friend, device_id_type=MESH)

    acc[...] = jnp.zeros_like(acc)

    load_tensor.wait()
    for q in range(4):
        for n, b in enumerate(WHOLE[q]):
            scale = tmask[0, b].astype(jnp.float32)
            block = tensor[b * BLK:(b + 1) * BLK, :].astype(jnp.float32)
            bpart[q, n * BLK:(n + 1) * BLK, :] = (block * scale).astype(jnp.bfloat16)
        b = SHARED[q]
        first = b * BLK + SUB * LAST[q]
        block = tensor[first:first + SUB, :].astype(jnp.float32) * tmask[0, b].astype(jnp.float32)
        bpart[q, 3 * BLK:, :] = block.astype(jnp.bfloat16)
    pl.semaphore_wait(barrier, len(friends))
    pltpu.make_async_copy(bpart.at[x], by.at[y, x], y_recv.at[y, x]).start()
    for d in (2, 1, 3):
        q = (x + d) % 4
        remote(bpart.at[q], by.at[y, x], bx_send.at[d], y_recv.at[y, x], at(q, y, z, core)).start()


    load_green.wait()
    left = lax.broadcasted_iota(jnp.int32, (SUB, BLK), 1) < SUB
    for q in range(4):
        for n, b in enumerate(WHOLE[q]):
            scale = gmask[0, b].astype(jnp.float32)
            block = green[:, b * BLK:(b + 1) * BLK].astype(jnp.float32)
            gpart[q, n * BLK:(n + 1) * BLK, :] = (block * scale).astype(jnp.bfloat16)
        b = SHARED[q]
        block = green[:, b * BLK:(b + 1) * BLK].astype(jnp.float32) * gmask[0, b].astype(jnp.float32)
        top, bottom = block[:SUB], block[SUB:]
        if LAST[q]:
            both = jnp.where(left, pltpu.roll(top, SUB, 1), bottom)
        else:
            both = jnp.where(left, top, pltpu.roll(bottom, SUB, 1))
        gpart[q, 3 * BLK:, :] = both.astype(jnp.bfloat16)

    lands = (
        ((z0.at[4], 0, PART, 0),),
        ((z1.at[0], 0, PART, 1),),
        tuple((ref.at[0], *cut, 2 + n) for n, (ref, cut) in enumerate(zip((z2a, z2b, z2c), CUTS))),
        ((z3.at[0], 0, PART, 5),),
    )
    for p in range(4):
        @pl.when(x == p)
        def _():
            for dst, first, count, s in lands[p]:
                pltpu.make_async_copy(gpart.at[p, pl.ds(first, count)], dst, gx_recv.at[s]).start()
            for d in (2, 1, 3):
                q = (p + d) % 4
                for dst, first, count, s in lands[p]:
                    remote(gpart.at[q, pl.ds(first, count)], dst, gx_send.at[d, s], gx_recv.at[s], at(q, y, z, core)).start()

    conveyors = (
        (1, 2, jnp.where(b_down == 1, far_down, far_up), lambda t: z2b.at[t], 1 - 2 * b_down),
        (0, 2, jnp.where(a_down == 1, far_down, far_up), lambda t: z2a.at[t], 1 - 2 * a_down),
        (2, 2, far_up, lambda t: z2c.at[t], 1),
        (3, 1, n1, lambda t: z1.at[t], -1),
        (4, 3, n3, lambda t: z3.at[t], 1),
        (5, 0, n0d, lambda t: z0.at[4 - t], -1),
        (6, 0, n0u, lambda t: z0.at[4 + t], 1),
    )

    def jump_of(hops):
        return jnp.maximum(hops - 1 - odd, 0)

    def hop(number, slot, way, t, by_hops):
        device = at(x, y, (z + way * by_hops + 16) % 16, core)
        return remote(slot(t), slot(t + by_hops), z_send.at[number, t + by_hops], z_recv.at[number, t + by_hops], device)

    def z_first(p):
        for dst, first, count, s in lands[p]:
            pltpu.make_async_copy(dst, dst, gx_recv.at[s]).wait()
        for number, part, hops, slot, way in conveyors:
            if part == p:
                @pl.when(hops > 0)
                def _():
                    hop(number, slot, way, 0, jnp.maximum(jump_of(hops), 1)).start()

    def z_step(step, parts):
        for number, part, hops, slot, way in conveyors:
            t = jump_of(hops) + step
            if part in parts:
                @pl.when(jnp.logical_and(t > 0, t <= hops))
                def _():
                    hop(number, slot, way, t - 1, 1).wait_recv()

                    @pl.when(t < hops)
                    def _():
                        hop(number, slot, way, t, 1).start()

    def codes_of(pair, way):
        code = 0
        for m in range(4):
            for c in range(2):
                here = jnp.logical_and(z % 4 == m, core == c)
                code = code + jnp.where(here, HOP_CODES[pair][way][m][c], 0)
        return code

    codes = tuple(tuple(codes_of(pair, way) for way in range(2)) for pair in range(2))

    def y_hops(pair, way, o):
        return lax.shift_right_logical(codes[pair][way], 3 * ((o + 4 * core) % 8)) % 8

    def wanted(way, o, t):
        origin = (o + 4 * core) % 8
        place = (origin + (t if way == 0 else 8 - t)) % 8
        e = (place - origin + z + 16) % 4
        third = jnp.logical_and(origin >= 4, e == 3 - core)
        return jnp.logical_and(place < 4, jnp.logical_or(e < 2, third))

    def y_hop(way, t, o, p, hops):
        by_hops = hops - t
        for d in (4, 3, 2, 1):
            by_hops = jnp.where(jnp.logical_and(t + d <= hops, wanted(way, o, t + d)), d, by_hops)
        device = at(x, (y + (by_hops if way == 0 else 8 - by_hops)) % 8, z, core)
        return remote(by.at[o, p], by.at[o, p], y_send.at[way, t, p], y_recv.at[o, p], device)

    e_mate = (2 * half - 1 - 1) // 2

    def piece_of(o):
        return 2 * ((low + z - e_mate - o % 4 + 16) % 4) + o // 4 - 1

    def hand(o, p):
        piece = piece_of(o)
        return remote(by.at[o, p], by.at[8 + piece, p], c_send.at[o, p], c_recv.at[piece, p], mate)

    def handed(o):
        piece = piece_of(o)
        return jnp.logical_and(core == half, jnp.logical_and(piece >= 0, piece <= 3))

    def y_step(a, t):
        p = (x + ORDER[a]) % 4

        def arrived(o):
            pltpu.make_async_copy(by.at[o, p], by.at[o, p], y_recv.at[o, p]).wait()

        @pl.when(t == 0)
        def _():
            arrived(y)
            for way in range(2):
                hops = y_hops(a // 2, way, y)

                @pl.when(hops > 0)
                def _():
                    y_hop(way, 0, y, p, hops).start()

            @pl.when(jnp.logical_and(handed(y), half == core))
            def _():
                hand(y, p).start()

        @pl.when(jnp.logical_and(t > 0, t <= Y_HOPS))
        def _():
            for way in range(2):
                o = (y + (8 - t if way == 0 else t)) % 8
                hops = y_hops(a // 2, way, o)

                @pl.when(jnp.logical_and(hops >= t, wanted(way, o, t)))
                def _():
                    arrived(o)

                    @pl.when(hops > t)
                    def _():
                        y_hop(way, t, o, p, hops).start()

                    @pl.when(handed(o))
                    def _():
                        hand(o, p).start()

    y_step(0, 0)
    for p in range(4):
        pl.when(x == p)(lambda p=p: z_first(p))

    def y_all(t, carry):
        for a in range(4):
            y_step(a, t - a)

        @pl.when(t == 2)
        def _():
            for p in range(4):
                pl.when(x != p)(lambda p=p: z_first(p))

        @pl.when(t == 5)
        def _():
            z_step(0, (0, 3))

        @pl.when(t == 6)
        def _():
            z_step(0, (1,))
            z_step(1, (0, 3))

        @pl.when(t == 7)
        def _():
            z_step(0, (2,))
            z_step(1, (1,))
            z_step(2, (0, 3))

        return carry

    lax.fori_loop(1, Y_HOPS + 4, y_all, 0)

    @pl.when(odd == 1)
    def _():
        for piece in range(4):
            for p in range(4):
                pltpu.make_async_copy(by.at[8 + piece, p], by.at[8 + piece, p], c_recv.at[piece, p]).wait()

    nothing = jnp.zeros((SUB, BLK), jnp.bfloat16)

    def one(p, n):
        e = n - down
        if p == 0:
            part = z0[4 - low + e]
        elif p == 1:
            part = z1[4 + low - e]
        elif p == 2:
            h_up, h_down = 8 - low + e, 8 + low - e
            part = jnp.concatenate([z2a[jnp.where(a_down == 1, h_down, h_up)], z2b[jnp.where(b_down == 1, h_down, h_up)],
                                    z2c[h_up]], axis=0)
        else:
            part = z3[4 - low + e]
        wide = jnp.concatenate([part[:BLK], part[BLK:2 * BLK], part[2 * BLK:3 * BLK]], axis=1)
        rest = part[3 * BLK:]
        place = ((low + 4 * p + z - e + 16) % 16) // 4
        for hj in range(2):
            s = core + hj - half + 2 * e

            @pl.when(jnp.logical_and(s >= 0, s <= 3))
            def _():
                where = jnp.where(odd == 1, 8 + 2 * n + hj - 1, 4 * hj + (low + z - e + 16) % 4)
                other = by[where, place]
                last = other[3 * BLK:]
                ends = jnp.concatenate([jnp.concatenate([last, nothing], axis=0), jnp.concatenate([nothing, last], axis=0)], axis=1)
                total = jnp.dot(wide, other[:3 * BLK], preferred_element_type=jnp.float32)
                pair = jnp.dot(rest, ends, preferred_element_type=jnp.float32)
                acc[p, hj] += total + jnp.concatenate([pair[:, :BLK], pair[:, BLK:]], axis=0)

    def give(p, hj):
        return remote(acc.at[p, hj], got.at[2 * x + hj], o_send.at[p, hj], o_recv.at[2 * x + hj], at(p, y, z, core))

    def give_owner(p, hj):
        return remote(acc.at[p, hj], got.at[2 * x + half], o_send.at[p, hj], o_recv.at[2 * x + half], at(p, 4 * hj + low, z, core))

    direct = x < 0
    for p in DIRECT:
        direct = jnp.logical_or(direct, x == p)

    swap = remote(acc.at[x, 1 - half], got.at[8], o_send.at[x, half], o_recv.at[8], at(x, (y + 4) % 8, z, core))

    def took(n):
        pltpu.make_async_copy(got.at[n], got.at[n], o_recv.at[n]).wait()

    def products(p):
        one(p, 0)
        one(p, 1)

        @pl.when(odd == 1)
        def _():
            one(p, 2)

        for hj in range(2):
            if p in DIRECT:
                @pl.when(jnp.logical_or(x != p, half != hj))
                def _():
                    give_owner(p, hj).start()
            else:
                @pl.when(x != p)
                def _():
                    give(p, hj).start()

    def sum_x():
        for d in (1, 3, 2):
            for hj in range(2):
                n = 2 * ((x + d) % 4) + hj
                took(n)
                acc[x, hj] += got[n]
        swap.start()

    products(0)
    products(3)
    z_step(1, (2,))
    z_step(2, (1,))
    products(1)
    z_step(2, (2,))
    products(2)
    pl.when(jnp.logical_not(direct))(sum_x)

    @pl.when(jnp.logical_not(direct))
    def _():
        took(8)
        out[...] = (acc[x, half] + got[8]).astype(jnp.bfloat16)

    @pl.when(direct)
    def _():
        total = acc[x, half]
        for d in range(1, 8):
            n = (2 * x + half + d) % 8
            took(n)
            total = total + got[n]
        out[...] = total.astype(jnp.bfloat16)

    for p in range(4):
        for hj in range(2):
            if p in DIRECT:
                @pl.when(jnp.logical_or(x != p, half != hj))
                def _():
                    give_owner(p, hj).wait_send()
            else:
                @pl.when(x != p)
                def _():
                    give(p, hj).wait_send()

        @pl.when(x == p)
        def _():
            for d in (1, 2, 3):
                for dst, first, count, s in lands[p]:
                    remote(gpart.at[p, pl.ds(first, count)], dst, gx_send.at[d, s], gx_recv.at[s], mate).wait_send()
    for d in (1, 2, 3):
        remote(bpart.at[x], by.at[y, x], bx_send.at[d], y_recv.at[y, x], mate).wait_send()

    pl.when(jnp.logical_not(direct))(swap.wait_send)
    for number, part, hops, slot, way in conveyors:
        jump = jump_of(hops)

        @pl.when(hops > 0)
        def _():
            hop(number, slot, way, 0, jnp.maximum(jump, 1)).wait_send()

        for step in range(3):
            t = jump + step

            @pl.when(jnp.logical_and(t > 0, t < hops))
            def _():
                hop(number, slot, way, t, 1).wait_send()

    def drain(t, carry):
        for a in range(4):
            p = (x + ORDER[a]) % 4
            for way in range(2):
                o = (y + (8 - t if way == 0 else t)) % 8
                hops = y_hops(a // 2, way, o)

                @pl.when(jnp.logical_and(hops > t, jnp.logical_or(t == 0, wanted(way, o, t))))
                def _():
                    y_hop(way, t, o, p, hops).wait_send()

                reached = hops >= t if way == 0 else jnp.logical_and(hops >= t, t > 0)

                @pl.when(jnp.logical_and(handed(o), reached))
                def _():
                    hand(o, p).wait_send()
        return carry

    lax.fori_loop(0, Y_HOPS + 1, drain, 0)


def shards(green, green_mask, tensor, tensor_mask):
    vmem, smem, hbm = (pl.BlockSpec(memory_space=space) for space in (pltpu.VMEM, pltpu.SMEM, pltpu.HBM))
    half, single, dma = jnp.bfloat16, jnp.float32, pltpu.SemaphoreType.DMA
    slots = Z_HOPS + 1
    return pl.pallas_call(
        kernel,
        name="window",
        out_shape=jax.ShapeDtypeStruct((BLK, BLK), half),
        in_specs=[hbm, smem, hbm, smem],
        out_specs=vmem,
        scratch_shapes=[
            pltpu.VMEM((BLK, WIDTH), half), pltpu.VMEM((WIDTH, BLK), half),
            pltpu.VMEM((4, PART, BLK), half), pltpu.VMEM((4, PART, BLK), half),
            pltpu.VMEM((7, PART, BLK), half), pltpu.VMEM((9, PART, BLK), half),
            *(pltpu.VMEM((slots, count, BLK), half) for _, count in CUTS),
            pltpu.VMEM((7, PART, BLK), half), pltpu.VMEM((12, 4, PART, BLK), half),
            pltpu.VMEM((4, 2, BLK, BLK), single), pltpu.VMEM((9, BLK, BLK), single),
            dma((2,)), dma((4, 6)), dma((6,)), dma((4,)), dma((7, slots)), dma((7, slots)),
            dma((2, Y_HOPS + 1, 4)), dma((8, 4)), dma((8, 4)), dma((4, 4)), dma((4, 2)), dma((9,)),
        ],
        compiler_params=pltpu.CompilerParams(collective_id=0, has_side_effects=True, vmem_limit_bytes=60 << 20),
        cost_estimate=pl.CostEstimate(flops=8 * BLK * BLK * WIDTH, bytes_accessed=4 * BLK * WIDTH, transcendentals=0),
    )(green, green_mask, tensor, tensor_mask.T)


def solution(mesh):
    spec = P("row", "col")
    return jax.shard_map(shards, mesh=mesh, in_specs=(spec,) * 4, out_specs=spec, check_vma=False)
```
